256 devices in a mesh: dom: 64 (over y_lo, x, z), edge: 4 (over y_hi, core).
Axes of the slice: x: 4, y: 4 (y_hi: 2, y_lo: 2; y = y_hi * 2 + y_lo), z: 8, core: 2. Of those that a mesh axis runs over, the one named last changes fastest.
Arguments:
- embedding: float32 [16384, 800], P('dom')
- adagrad_state: float32 [16384], P('dom'), may hold values from 0.05 to 1
- relation_table: bfloat16 [128, 800], replicated, may hold values from -4 to 4
- source_row: int32 [2, 64, 1024], P(None, 'dom', 'edge'), may hold values from 0 to 255
- target_row: int32 [2, 64, 1024], P(None, 'dom', 'edge'), may hold values from 0 to 255
- relation_id: int32 [2, 64, 1024], P(None, 'dom', 'edge'), may hold values from 0 to 127
- negative_row: int32 [2, 64, 4, 1024], P(None, 'dom', 'edge'), may hold values from 0 to 255
Outputs:
- new_embedding: float32 [16384, 800], P('dom')
- new_state: float32 [16384], P('dom')
The draws below stay inside these ranges and needn't reach their ends.
All inputs are finite; a program needn't handle non-finite values.
Results may differ from the reference program's by a relative error of at most 0.008.
Values may be sent and summed in bfloat16 or wider, within the bound.
A program may use at most 64 MiB of HBM per device.

```python
import math
import jax
import jax.numpy as jnp
from jax import lax

DIM = 400
R_DEV = 256
GROUP = 256
NEG = 1024
REL = 128
ROUNDS = 2
ENTITIES = 16384
BUCKET = 1024
N_DOM = 64


def draw_embedding(key, part):
    key = jax.random.fold_in(key, 11)
    first_key = jax.random.fold_in(key, 0)
    shape = (N_DOM * R_DEV, 2 * DIM)
    return 0.3 * jax.random.normal(first_key, shape, jnp.float32)


def with_ends(array, rng, least, top_value):
    spot = [jax.random.randint(jax.random.fold_in(rng, axis), (), 0, length) for axis, length in enumerate(array.shape)]
    longest = array.shape.index(max(array.shape))
    neighbour = spot[:longest] + [(spot[longest] + 1) % array.shape[longest]] + spot[longest + 1:]
    return array.at[tuple(spot)].set(least).at[tuple(neighbour)].set(top_value)


def levels(rng, dims, shards, smallest, top_value):
    def one(axis_at, shards_of):
        steps = jax.random.uniform(jax.random.fold_in(jax.random.fold_in(rng, 6), axis_at), (shards_of,), jnp.float32, smallest / len(shards), top_value / len(shards))
        return jnp.repeat(jnp.exp(steps), dims[axis_at] // shards_of).reshape((-1,) + (1,) * (len(dims) - axis_at - 1))

    loudness = one(*shards[0])
    for cut in shards[1:]:
        loudness = loudness * one(*cut)
    return loudness


def noise(stream_key, extent, scale, most, held_as=jnp.bfloat16):
    array = jax.random.normal(stream_key, extent, jnp.float32) * scale
    return jnp.minimum(jnp.maximum(array, -most), most).astype(held_as)


def setup_inputs(seed: int = 0) -> dict:
    keys = jax.random.split(jax.random.key(seed), 8)
    return {
        "embedding": draw_embedding(jax.random.fold_in(keys[7], 71), 0),
        "adagrad_state": jnp.clip(jnp.exp(math.log(1.0) - 2.9957323 * jax.random.uniform(keys[1], (ENTITIES,), jnp.float32) ** levels(keys[1], (ENTITIES,), ((0, 64),), -0.2, 0.2)), 0.05, 1.0),
        "relation_table": noise(keys[2], (REL, 2 * DIM), 1.0, 4.0),
        "source_row": with_ends(jax.random.randint(keys[3], (ROUNDS, N_DOM, BUCKET), 0, R_DEV), jax.random.fold_in(keys[3], 1), 0, R_DEV - 1).astype(jnp.int32),
        "target_row": with_ends(jax.random.randint(keys[4], (ROUNDS, N_DOM, BUCKET), 0, R_DEV), jax.random.fold_in(keys[4], 1), 0, R_DEV - 1).astype(jnp.int32),
        "relation_id": with_ends(jax.random.randint(keys[5], (ROUNDS, N_DOM, BUCKET), 0, REL), jax.random.fold_in(keys[5], 1), 0, REL - 1).astype(jnp.int32),
        "negative_row": with_ends(jax.random.randint(keys[6], (ROUNDS, N_DOM, BUCKET // GROUP, NEG), 0, R_DEV), jax.random.fold_in(keys[6], 1), 0, R_DEV - 1).astype(jnp.int32),
    }


learning_rate = 0.1

def complex_times(left, right):
    halfway = left.shape[-1] // 2
    left_real, left_imag = (left[..., :halfway], left[..., halfway:])
    right_real, right_imag = (right[..., :halfway], right[..., halfway:])
    return jnp.concatenate([left_real * right_real - left_imag * right_imag, left_real * right_imag + left_imag * right_real], axis=-1)

def conjugate_times(grad_value, right):
    halfway = grad_value.shape[-1] // 2
    grad_real, grad_imag = (grad_value[..., :halfway], grad_value[..., halfway:])
    right_real, right_imag = (right[..., :halfway], right[..., halfway:])
    return jnp.concatenate([grad_real * right_real + grad_imag * right_imag, grad_imag * right_real - grad_real * right_imag], axis=-1)

def group_terms(sources, targets, negatives, relations):
    product = complex_times(sources.astype(jnp.float32), relations).astype(jnp.bfloat16)
    product_wide = product.astype(jnp.float32)
    targets_wide = targets.astype(jnp.float32)
    positive = lax.optimization_barrier(jnp.sum(product_wide * targets_wide, axis=1))
    negative = lax.dot_general(product, negatives, (((1,), (1,)), ((), ())), preferred_element_type=jnp.float32)
    highest = jnp.maximum(lax.optimization_barrier(jnp.max(negative, axis=1)), positive)
    expo_neg = jnp.exp(negative - highest[:, None])
    expo_pos = jnp.exp(positive - highest)
    total = lax.optimization_barrier(jnp.sum(expo_neg, axis=1)) + expo_pos
    weights = (expo_neg / total[:, None]).astype(jnp.bfloat16)
    pull = expo_pos / total - 1.0
    grad_product = pull[:, None] * targets_wide + jnp.dot(weights, negatives, preferred_element_type=jnp.float32)
    grad_sources = conjugate_times(grad_product, relations)
    grad_targets = pull[:, None] * product_wide
    grad_negatives = lax.dot_general(weights, product, (((0,), (0,)), ((), ())), preferred_element_type=jnp.float32)
    return (grad_sources, grad_targets, grad_negatives)

def bucket_gradients(own_block, partner_block, relations, source_row, target_row, negative_row):
    groups = negative_row.shape[0]
    group_size = source_row.shape[0] // groups
    feature_width = own_block.shape[1]
    row_count = own_block.shape[0]
    sources = jnp.take(own_block, source_row, axis=0).reshape(groups, group_size, feature_width)
    targets = jnp.take(partner_block, target_row, axis=0).reshape(groups, group_size, feature_width)
    relations = relations.reshape(groups, group_size, feature_width)

    def per_group(group_items):
        source_part, target_part, relation_part, negative_index = group_items
        negatives = jnp.take(partner_block, negative_index, axis=0)
        return group_terms(source_part, target_part, negatives, relation_part)
    grad_sources, grad_targets, grad_negatives = lax.map(per_group, (sources, targets, relations, negative_row))
    grad_source = jax.ops.segment_sum(grad_sources.reshape(-1, feature_width), source_row, num_segments=row_count)
    grad_target = jax.ops.segment_sum(grad_targets.reshape(-1, feature_width), target_row, num_segments=row_count)
    grad_target = grad_target + jax.ops.segment_sum(grad_negatives.reshape(-1, feature_width), negative_row.reshape(-1), num_segments=row_count)
    return (grad_source, grad_target)

def adagrad_step(weights, state, gradient):
    new_state = state + lax.optimization_barrier(jnp.mean(gradient * gradient, axis=1))
    return (weights - learning_rate * gradient / jnp.sqrt(new_state)[:, None], new_state)

def reference(embedding, adagrad_state, relation_table, source_row, target_row, relation_id, negative_row):
    weights, state = (embedding, adagrad_state)
    for round_index in range(ROUNDS):
        blocks = weights.astype(jnp.bfloat16).reshape(N_DOM, R_DEV, 2 * DIM)
        partners = jnp.roll(blocks, round_index + 1, axis=0)

        def one_bucket(bucket_items):
            own_block, partner_block, sources, targets, relations, negatives = bucket_items
            relation_rows = jnp.take(relation_table, relations, axis=0).astype(jnp.float32)
            return bucket_gradients(own_block, partner_block, relation_rows, sources, targets, negatives)
        grad_source, grad_target = lax.map(one_bucket, (blocks, partners, source_row[round_index], target_row[round_index], relation_id[round_index], negative_row[round_index]))
        gradient = grad_source + jnp.roll(grad_target, -(round_index + 1), axis=0)
        weights, state = adagrad_step(weights, state, gradient.reshape(N_DOM * R_DEV, 2 * DIM))
    return (weights, state)
```

```python
import functools

import jax
import jax.numpy as jnp
from jax import lax
from jax.experimental import pallas as pl
from jax.experimental.pallas import tpu as pltpu
from jax.sharding import PartitionSpec as P

MESH = pl.DeviceIdType.MESH
F32 = jnp.float32
BF16 = jnp.bfloat16

learning_rate = 0.1
ROWS = 256
HALF = 128
GROUPS = 4
E = 256
WIDE = 896
FULL = 1024


def lanes(shape):
    return lax.broadcasted_iota(jnp.int32, shape, 1)


def arrange(tiles):
    lane = lanes(tiles[0].shape)
    moved = [pltpu.roll(t, 112, 1) for t in tiles[3:7]]
    imag = [jnp.where(lane < 112, moved[j], moved[j + 1]) for j in range(3)]
    tail = jnp.where(lane < 16, tiles[3], jnp.where(lane < 32, tiles[6], 0.0))
    return tiles[:3] + imag + [tail]


def swapped(tail):
    lane = lanes(tail.shape)
    return jnp.where(
        lane < 16, pltpu.roll(tail, 112, 1), jnp.where(lane < 32, pltpu.roll(tail, 16, 1), 0.0)
    )


def natural_tiles(ref, rows):
    parts = [ref[rows, 128 * j : 128 * (j + 1)].astype(F32) for j in range(6)]
    last = ref[rows, 768:800].astype(F32)
    return parts + [jnp.concatenate([last, jnp.zeros((last.shape[0], 96), F32)], axis=1)]


def dot(a, b, ca, cb):
    return lax.dot_general(a, b, (((ca,), (cb,)), ((), ())), preferred_element_type=F32)


def kernel(
    n_dom,
    emb, state, rel, src, tgt, rid, neg,
    out_w, out_s,
    nat, statev, relv, srcv, tgtv, ridv, negv,
    pack, idx, buf, w, scol, rtab, r, q, ots, lc, gt, gs, xs, xr,
    load_sem, row_send, row_recv, idx_send, idx_recv, x_send, x_recv,
):
    d = lax.axis_index("dom")
    e = lax.axis_index("edge")
    core = lax.rem(e, 2)
    plane = e - core
    sibling = plane + (1 - core)
    up = [lax.rem(d + k + 1, n_dom) for k in range(2)]
    down = [lax.rem(d + n_dom - k - 1, n_dom) for k in range(2)]

    barrier = pltpu.get_barrier_semaphore()

    def tell(dom, edge):
        pl.semaphore_signal(barrier, inc=1, device_id=(dom, edge), device_id_type=MESH)

    @pl.when(core == 0)
    def _():
        for k in range(2):
            tell(down[k], plane)
            tell(down[k], plane + 1)
        tell(d, sibling)
        tell(d, 2 - plane)
        tell(d, 3 - plane)

    @pl.when(core == 1)
    def _():
        for k in range(2):
            for g in range(GROUPS):
                tell(up[k], g)
        tell(d, sibling)

    loads = [
        pltpu.make_async_copy(a, b, load_sem.at[i])
        for i, (a, b) in enumerate(
            zip((src, tgt, rid, neg, emb, state, rel), (srcv, tgtv, ridv, negv, nat, statev, relv))
        )
    ]
    for c in loads:
        c.start()
    for c in loads[:4]:
        c.wait()
    for k in range(2):
        pack[k, 0:1, :] = srcv[k]
        pack[k, 1:2, :] = tgtv[k]
        pack[k, 2:3, :] = ridv[k]
        for j in range(4):
            pack[k, 3 + j : 4 + j, :] = negv[k, 0, :, 256 * j : 256 * (j + 1)]

    @pl.when(core == 0)
    def _():
        for k in range(2):
            idx[k, e] = pack[k]

    for c in loads[4:]:
        c.wait()
    tiles = arrange(natural_tiles(nat, slice(None)))
    for j in range(7):
        w[:, 128 * j : 128 * (j + 1)] = tiles[j]
        buf[0, core, :, 128 * j : 128 * (j + 1)] = tiles[j].astype(BF16)
    buf[0, core, :, WIDE:FULL] = swapped(tiles[6]).astype(BF16)

    pl.semaphore_wait(barrier, 8)

    def idx_copy(k, j, group, dom, edge):
        return pltpu.make_async_remote_copy(
            src_ref=pack.at[k],
            dst_ref=idx.at[k, group],
            send_sem=idx_send.at[k, j],
            recv_sem=idx_recv.at[k, group],
            device_id=(dom, edge),
            device_id_type=MESH,
        )

    def idx_sends(k, act):
        for h in range(2):
            pl.when(e != 2 * h)(lambda h=h: act(idx_copy(k, h, e, d, 2 * h)))
            act(idx_copy(k, 2 + h, e, down[k], 2 * h + 1))

    def idx_waits(k):
        for g in range(GROUPS):
            pl.when(e != g + 4 * core)(lambda g=g: idx_copy(k, 0, g, d, sibling).wait_recv())

    mine = pl.ds(pl.multiple_of(core * HALF, HALF), HALF)
    other = pl.ds(pl.multiple_of((1 - core) * HALF, HALF), HALF)

    def row_copy(k, way):
        return pltpu.make_async_remote_copy(
            src_ref=buf.at[k, core, mine, pl.ds(0, WIDE)],
            dst_ref=buf.at[k, 1 - way, mine, pl.ds(0, WIDE)],
            send_sem=row_send.at[k, way],
            recv_sem=row_recv.at[k, core],
            device_id=((up[k], plane), (down[k], plane + 1))[way],
            device_id_type=MESH,
        )

    def row_arrival(k, half):
        part = pl.ds(half * HALF, HALF)
        return pltpu.make_async_remote_copy(
            src_ref=buf.at[k, core, part, pl.ds(0, WIDE)],
            dst_ref=buf.at[k, 1 - core, part, pl.ds(0, WIDE)],
            send_sem=row_send.at[k, half],
            recv_sem=row_recv.at[k, half],
            device_id=(d, sibling),
            device_id_type=MESH,
        )

    def x_copy(k, j):
        part = (other, mine)[j]
        return pltpu.make_async_remote_copy(
            src_ref=xs.at[k, part],
            dst_ref=xr.at[k, part],
            send_sem=x_send.at[k, j],
            recv_sem=x_recv.at[k, j],
            device_id=(d, sibling),
            device_id_type=MESH,
        )

    idx_sends(0, lambda c: c.start())
    row_copy(0, 0).start()
    row_copy(0, 1).start()
    idx_sends(1, lambda c: c.start())

    tiles = arrange(natural_tiles(relv, slice(None)))
    lane = lanes((128, 128))
    swap = swapped(tiles[6])
    for j in range(6):
        rtab[:, 128 * j : 128 * (j + 1)] = tiles[j].astype(BF16)
    rtab[:, 768:896] = jnp.where(lane < 16, tiles[6], swap).astype(BF16)
    rtab[:, 896:1024] = jnp.where(lane < 16, -swap, tiles[6]).astype(BF16)
    eye = lax.broadcasted_iota(jnp.int32, (ROWS, ROWS), 0) == lanes((ROWS, ROWS))
    row = jnp.reshape(statev[...], (1, ROWS))
    scol[...] = jnp.sum(jnp.where(eye, row, 0.0), axis=1, keepdims=True)

    def prepare(k):
        idx_waits(k)
        at = lax.broadcasted_iota(jnp.int32, (ROWS, E), 0)
        for g in range(GROUPS):
            cols = slice(g * E, (g + 1) * E)
            ots[:, cols] = jnp.where(at == idx[k, g, 0:1, :], 1.0, 0.0).astype(BF16)
            count = jnp.zeros((ROWS, E), F32)
            for j in range(4):
                count += jnp.where(at == idx[k, g, 3 + j : 4 + j, :], 1.0, 0.0)
            lc[:, g : g + 1] = jnp.log(jnp.sum(count, axis=1, keepdims=True))
            kind = jnp.where(at[:HALF] == idx[k, g, 2:3, :], 1.0, 0.0).astype(BF16)
            r[cols, :] = dot(kind, rtab[...], 0, 0).astype(BF16)

    def products(k):
        for g in range(GROUPS):
            cols = slice(g * E, (g + 1) * E)
            s = dot(ots[:, cols], buf[k, 0], 0, 0)
            rr = r[cols, :].astype(F32)
            re = s[:, :384] * rr[:, :384] - s[:, 384:768] * rr[:, 384:768]
            im = s[:, :384] * rr[:, 384:768] + s[:, 384:768] * rr[:, :384]
            tail = s[:, 768:896] * rr[:, 768:896] + s[:, 896:] * rr[:, 896:]
            q[cols, 0:384] = re.astype(BF16)
            q[cols, 384:768] = im.astype(BF16)
            q[cols, 768:896] = tail.astype(BF16)

    def pulls(k):
        at = lax.broadcasted_iota(jnp.int32, (ROWS, E), 0)
        for g in range(GROUPS):
            cols = slice(g * E, (g + 1) * E)
            score = dot(buf[k, 1, :, 0:WIDE], q[cols, :], 1, 1)
            hit = at == idx[k, g, 1:2, :]
            pos = jnp.sum(jnp.where(hit, score, 0.0), axis=0, keepdims=True)
            z = score + lc[:, g : g + 1]
            top = jnp.maximum(jnp.max(z, axis=0, keepdims=True), pos)
            ez = jnp.exp(z - top)
            ep = jnp.exp(pos - top)
            inv = 1.0 / (jnp.sum(ez, axis=0, keepdims=True) + ep)
            pull = ep * inv - 1.0
            gt[:, cols] = (ez * inv + jnp.where(hit, pull, 0.0)).astype(BF16)

    def source_terms(k):
        for g in range(GROUPS):
            cols = slice(g * E, (g + 1) * E)
            gq = dot(gt[:, cols], buf[k, 1], 0, 0)
            rr = r[cols, :].astype(F32)
            re = gq[:, :384] * rr[:, :384] + gq[:, 384:768] * rr[:, 384:768]
            im = gq[:, 384:768] * rr[:, :384] - gq[:, :384] * rr[:, 384:768]
            tail = gq[:, 768:896] * rr[:, 768:896] - gq[:, 896:] * rr[:, 896:]
            gs[cols, 0:384] = re.astype(BF16)
            gs[cols, 384:768] = im.astype(BF16)
            gs[cols, 768:896] = tail.astype(BF16)

    def update(k, part, last):
        g = xs[k, part].astype(F32) + xr[k, part].astype(F32)
        new_s = scol[part] + jnp.sum(g * g, axis=1, keepdims=True) * (1.0 / 800.0)
        new_w = w[part] - g * (learning_rate * lax.rsqrt(new_s))
        scol[part] = new_s
        if not last:
            w[part] = new_w
            buf[1, core, part, 0:WIDE] = new_w.astype(BF16)
            buf[1, core, part, WIDE:FULL] = swapped(new_w[:, 768:896]).astype(BF16)
        else:
            t = [new_w[:, 128 * j : 128 * (j + 1)] for j in range(7)]
            moved = [pltpu.roll(v, 16, 1) for v in t[3:6]]
            lane = lanes(t[0].shape)
            for j in range(3):
                out_w[part, 128 * j : 128 * (j + 1)] = t[j]
            out_w[part, 384:512] = jnp.where(lane < 16, t[6], moved[0])
            out_w[part, 512:640] = jnp.where(lane < 16, moved[0], moved[1])
            out_w[part, 640:768] = jnp.where(lane < 16, moved[1], moved[2])
            out_w[part, 768:800] = jnp.where(lane < 16, moved[2], t[6])[:, :32]

    for k in range(2):
        prepare(k)
        pl.when(core == 0)(lambda k=k: products(k))
        for half in range(2):
            row_arrival(k, half).wait_recv()
        tail = buf[k, 1 - core, :, 768:896].astype(F32)
        buf[k, 1 - core, :, WIDE:FULL] = swapped(tail).astype(BF16)
        pl.when(core == 1)(lambda k=k: products(k))
        pulls(k)
        pl.when(core == 0)(lambda k=k: source_terms(k))
        for j, part in enumerate((other, mine)):

            @pl.when(core == 0)
            def _():
                xs[k, part] = dot(ots[part, :], gs[...], 1, 0).astype(BF16)

            @pl.when(core == 1)
            def _():
                xs[k, part] = dot(gt[part, :], q[...], 1, 0).astype(BF16)

            x_copy(k, j).start()
        x_copy(k, 0).wait_recv()
        update(k, mine, k == 1)
        if k == 0:
            row_copy(1, 0).start()
            row_copy(1, 1).start()
        x_copy(k, 1).wait_recv()
        update(k, other, k == 1)

    out_s[...] = jnp.reshape(jnp.sum(jnp.where(eye, scol[...], 0.0), axis=0, keepdims=True), (ROWS,))
    for k in range(2):
        idx_sends(k, lambda c: c.wait_send())
        for j in range(2):
            row_copy(k, j).wait_send()
            x_copy(k, j).wait_send()


def solution(mesh):
    n_dom = mesh.shape["dom"]

    def body(embedding, adagrad_state, relation_table, source_row, target_row, relation_id, negative_row):
        any_space = pl.BlockSpec(memory_space=pl.ANY)
        vmem = pl.BlockSpec(memory_space=pltpu.VMEM)
        dma = pltpu.SemaphoreType.DMA
        return pl.pallas_call(
            functools.partial(kernel, n_dom),
            out_shape=(
                jax.ShapeDtypeStruct(embedding.shape, F32),
                jax.ShapeDtypeStruct(adagrad_state.shape, F32),
            ),
            in_specs=[any_space] * 7,
            out_specs=(vmem, vmem),
            scratch_shapes=[
                pltpu.VMEM(embedding.shape, F32),
                pltpu.VMEM(adagrad_state.shape, F32),
                pltpu.VMEM(relation_table.shape, BF16),
                pltpu.VMEM(source_row.shape, jnp.int32),
                pltpu.VMEM(target_row.shape, jnp.int32),
                pltpu.VMEM(relation_id.shape, jnp.int32),
                pltpu.VMEM(negative_row.shape, jnp.int32),
                pltpu.VMEM((2, 8, E), jnp.int32),
                pltpu.VMEM((2, GROUPS, 8, E), jnp.int32),
                pltpu.VMEM((2, 2, ROWS, FULL), BF16),
                pltpu.VMEM((ROWS, WIDE), F32),
                pltpu.VMEM((ROWS, 1), F32),
                pltpu.VMEM((128, FULL), BF16),
                pltpu.VMEM((GROUPS * E, FULL), BF16),
                pltpu.VMEM((GROUPS * E, WIDE), BF16),
                pltpu.VMEM((ROWS, GROUPS * E), BF16),
                pltpu.VMEM((ROWS, GROUPS), F32),
                pltpu.VMEM((ROWS, GROUPS * E), BF16),
                pltpu.VMEM((GROUPS * E, WIDE), BF16),
                pltpu.VMEM((2, ROWS, WIDE), BF16),
                pltpu.VMEM((2, ROWS, WIDE), BF16),
                dma((7,)),
                dma((2, 2)),
                dma((2, 2)),
                dma((2, 4)),
                dma((2, 4)),
                dma((2, 2)),
                dma((2, 2)),
            ],
            compiler_params=pltpu.CompilerParams(
                collective_id=0, has_side_effects=True, vmem_limit_bytes=48 * 2**20
            ),
        )(embedding, adagrad_state, relation_table, source_row, target_row, relation_id, negative_row)

    in_specs = (
        P("dom", None),
        P("dom"),
        P(),
        P(None, "dom", "edge"),
        P(None, "dom", "edge"),
        P(None, "dom", "edge"),
        P(None, "dom", "edge", None),
    )
    out_specs = (P("dom", None), P("dom"))
    return jax.shard_map(body, mesh=mesh, in_specs=in_specs, out_specs=out_specs, check_vma=False)
```

```python
import functools

import jax
import jax.numpy as jnp
from jax import lax
from jax.experimental import pallas as pl
from jax.experimental.pallas import tpu as pltpu
from jax.sharding import PartitionSpec as P

MESH = pl.DeviceIdType.MESH
F32 = jnp.float32
BF16 = jnp.bfloat16

learning_rate = 0.1
ROWS = 256
HALF = 128
GROUPS = 4
E = 256
COLS = 800

CHUNKS = ((0, 208, 0), (416, 192, 208))
NATURAL = [(a, n, c) for a, n, c in CHUNKS] + [(a + n, n, c + 400) for a, n, c in CHUNKS]


def chunk(ch):
    a, n, _ = CHUNKS[ch]
    return pl.ds(a, 2 * n)


def parts(ch):
    a, n, _ = CHUNKS[ch]
    return pl.ds(a, n), pl.ds(a + n, n)


def dot(a, b, ca, cb):
    return lax.dot_general(a, b, (((ca,), (cb,)), ((), ())), preferred_element_type=F32)


def kernel(
    n_dom,
    emb, state, rel, src, tgt, rid, neg,
    out_w, out_s,
    w, statev, relv, srcv, tgtv, ridv, negv,
    pack, idx, buf, bt0, bt1, r, q, part, ots, lc, gt, gs, xs, xr,
    load_sem, emb_sem, rel_sem, row_send, row_recv, idx_send, idx_recv, x_send, x_recv,
):
    d = lax.axis_index("dom")
    e = lax.axis_index("edge")
    core = lax.rem(e, 2)
    plane = e - core
    sibling = plane + (1 - core)
    up = [lax.rem(d + k + 1, n_dom) for k in range(2)]
    down = [lax.rem(d + n_dom - k - 1, n_dom) for k in range(2)]
    mine = pl.ds(pl.multiple_of(core * HALF, HALF), HALF)
    other = pl.ds(pl.multiple_of((1 - core) * HALF, HALF), HALF)
    bt = (bt0, bt1)

    index_loads = [
        pltpu.make_async_copy(a, b, load_sem.at[i])
        for i, (a, b) in enumerate(((src, srcv), (tgt, tgtv), (rid, ridv), (neg, negv), (state, statev)))
    ]
    emb_loads = [
        pltpu.make_async_copy(emb.at[pl.ds(c, n), half], w.at[pl.ds(a, n), half], emb_sem.at[j, i])
        for j, half in enumerate((mine, other))
        for i, (a, n, c) in enumerate(NATURAL)
    ]
    rel_loads = [
        pltpu.make_async_copy(rel.at[pl.ds(c, n)], relv.at[pl.ds(a, n)], rel_sem.at[i])
        for i, (a, n, c) in enumerate(NATURAL)
    ]
    for c in index_loads[:4] + emb_loads[:4]:
        c.start()

    barrier = pltpu.get_barrier_semaphore()

    def tell(dom, edge):
        pl.semaphore_signal(barrier, inc=1, device_id=(dom, edge), device_id_type=MESH)

    @pl.when(core == 0)
    def _():
        for k in range(2):
            tell(down[k], plane)
            tell(down[k], plane + 1)
        tell(d, sibling)
        tell(d, 2 - plane)
        tell(d, 3 - plane)

    @pl.when(core == 1)
    def _():
        for k in range(2):
            for g in range(GROUPS):
                tell(up[k], g)
        tell(d, sibling)

    for c in emb_loads[4:] + rel_loads + index_loads[4:]:
        c.start()
    for c in index_loads[:4]:
        c.wait()
    for k in range(2):
        pack[k, 0:1, :] = srcv[k]
        pack[k, 1:2, :] = tgtv[k]
        pack[k, 2:3, :] = ridv[k]
        for j in range(4):
            pack[k, 3 + j : 4 + j, :] = negv[k, 0, :, 256 * j : 256 * (j + 1)]

    pl.semaphore_wait(barrier, 8)

    def idx_copy(k, j, group, dom, edge):
        return pltpu.make_async_remote_copy(
            src_ref=pack.at[k],
            dst_ref=idx.at[k, group],
            send_sem=idx_send.at[k, j],
            recv_sem=idx_recv.at[k, group],
            device_id=(dom, edge),
            device_id_type=MESH,
        )

    def idx_sends(k, act):
        for h in range(2):
            pl.when(e != 2 * h)(lambda h=h: act(idx_copy(k, h, e, d, 2 * h)))
            act(idx_copy(k, 2 + h, e, down[k], 2 * h + 1))

    def idx_waits(k):
        for g in range(GROUPS):
            pl.when(e != g + 4 * core)(lambda g=g: idx_copy(k, 0, g, d, sibling).wait_recv())

    def row_copy(k, way, ch):
        return pltpu.make_async_remote_copy(
            src_ref=buf.at[k, core, chunk(ch), mine],
            dst_ref=buf.at[k, 1 - way, chunk(ch), mine],
            send_sem=row_send.at[k, way, ch],
            recv_sem=row_recv.at[k, core, ch],
            device_id=((up[k], plane), (down[k], plane + 1))[way],
            device_id_type=MESH,
        )

    def row_arrival(k, half, ch):
        lane = pl.ds(half * HALF, HALF)
        return pltpu.make_async_remote_copy(
            src_ref=buf.at[k, core, chunk(ch), lane],
            dst_ref=buf.at[k, 1 - core, chunk(ch), lane],
            send_sem=row_send.at[k, half, ch],
            recv_sem=row_recv.at[k, half, ch],
            device_id=(d, sibling),
            device_id_type=MESH,
        )

    def x_copy(k, ch):
        return pltpu.make_async_remote_copy(
            src_ref=xs.at[k, chunk(ch)],
            dst_ref=xr.at[k, chunk(ch)],
            send_sem=x_send.at[k, ch],
            recv_sem=x_recv.at[k, ch],
            device_id=(d, sibling),
            device_id_type=MESH,
        )

    idx_sends(0, lambda c: c.start())
    for ch in range(2):
        emb_loads[ch].wait()
        emb_loads[2 + ch].wait()
        buf[0, core, chunk(ch), mine] = w[chunk(ch), mine].astype(BF16)
        for way in range(2):
            row_copy(0, way, ch).start()
    idx_sends(1, lambda c: c.start())

    @pl.when(core == 0)
    def _():
        for k in range(2):
            idx[k, e] = pack[k]

    for c in emb_loads[4:]:
        c.wait()
    buf[0, core, :, other] = w[:, other].astype(BF16)
    for c in rel_loads + index_loads[4:]:
        c.wait()

    def prepare(k):
        idx_waits(k)
        at = lax.broadcasted_iota(jnp.int32, (ROWS, E), 0)
        for g in range(GROUPS):
            cols = slice(g * E, (g + 1) * E)
            ots[:, cols] = jnp.where(at == idx[k, g, 0:1, :], 1.0, 0.0).astype(BF16)
            count = jnp.zeros((ROWS, E), F32)
            for j in range(4):
                count += jnp.where(at == idx[k, g, 3 + j : 4 + j, :], 1.0, 0.0)
            lc[:, g : g + 1] = jnp.log(jnp.sum(count, axis=1, keepdims=True))
            kind = jnp.where(at[:HALF] == idx[k, g, 2:3, :], 1.0, 0.0).astype(BF16)
            r[:, cols] = dot(relv[...], kind, 1, 0).astype(BF16)

    def flip(k, ch):
        bt[ch][...] = buf[k, 1, chunk(ch), :].T

    def products(k, ch):
        re, im = parts(ch)
        n = CHUNKS[ch][1]
        for g in range(GROUPS):
            cols = slice(g * E, (g + 1) * E)
            s = dot(buf[k, 0, chunk(ch), :], ots[:, cols], 1, 0)
            rr = r[re, cols].astype(F32)
            ri = r[im, cols].astype(F32)
            q[re, cols] = (s[:n] * rr - s[n:] * ri).astype(BF16)
            q[im, cols] = (s[:n] * ri + s[n:] * rr).astype(BF16)

    def scores():
        for g in range(GROUPS):
            cols = slice(g * E, (g + 1) * E)
            part[:, cols] = dot(bt0[...], q[chunk(0), cols], 1, 0)

    def pulls(k):
        at = lax.broadcasted_iota(jnp.int32, (ROWS, E), 0)
        for g in range(GROUPS):
            cols = slice(g * E, (g + 1) * E)
            score = part[:, cols] + dot(bt1[...], q[chunk(1), cols], 1, 0)
            hit = at == idx[k, g, 1:2, :]
            pos = jnp.sum(jnp.where(hit, score, 0.0), axis=0, keepdims=True)
            z = score + lc[:, g : g + 1]
            top = jnp.maximum(jnp.max(z, axis=0, keepdims=True), pos)
            ez = jnp.exp(z - top)
            ep = jnp.exp(pos - top)
            inv = 1.0 / (jnp.sum(ez, axis=0, keepdims=True) + ep)
            pull = ep * inv - 1.0
            gt[:, cols] = (ez * inv + jnp.where(hit, pull, 0.0)).astype(BF16)

    def source_terms(k, ch):
        re, im = parts(ch)
        n = CHUNKS[ch][1]
        for g in range(GROUPS):
            cols = slice(g * E, (g + 1) * E)
            gq = dot(buf[k, 1, chunk(ch), :], gt[:, cols], 1, 0)
            rr = r[re, cols].astype(F32)
            ri = r[im, cols].astype(F32)
            gs[re, cols] = (gq[:n] * rr + gq[n:] * ri).astype(BF16)
            gs[im, cols] = (gq[n:] * rr - gq[:n] * ri).astype(BF16)

    def update(k, lane):
        g = xs[k, :, lane].astype(F32) + xr[k, :, lane].astype(F32)
        new_s = statev[:, lane] + jnp.sum(g * g, axis=0, keepdims=True) * (1.0 / COLS)
        new_w = w[:, lane] - g * (learning_rate * lax.rsqrt(new_s))
        if k == 0:
            statev[:, lane] = new_s
            w[:, lane] = new_w
            buf[1, core, :, lane] = new_w.astype(BF16)
        else:
            out_s[:, lane] = new_s
            out_w[:, lane] = new_w

    for k in range(2):
        prepare(k)

        @pl.when(core == 0)
        def _():
            for ch in range(2):
                products(k, ch)

        @pl.when(core == 1)
        def _():
            for ch in range(2):
                flip(k, ch)

        for ch in range(2):
            for half in range(2):
                row_arrival(k, half, ch).wait_recv()
            pl.when(core == 0)(lambda: flip(k, ch))
            pl.when(core == 1)(lambda: products(k, ch))
            if ch == 0:
                scores()
        pulls(k)
        for ch in range(2):

            @pl.when(core == 0)
            def _():
                source_terms(k, ch)
                xs[k, chunk(ch)] = dot(gs[chunk(ch), :], ots[...], 1, 1).astype(BF16)

            @pl.when(core == 1)
            def _():
                xs[k, chunk(ch)] = dot(q[chunk(ch), :], gt[...], 1, 1).astype(BF16)

            x_copy(k, ch).start()
        for ch in range(2):
            x_copy(k, ch).wait_recv()
        update(k, mine)
        if k == 0:
            for ch in range(2):
                for way in range(2):
                    row_copy(1, way, ch).start()
        update(k, other)

    for k in range(2):
        idx_sends(k, lambda c: c.wait_send())
        for ch in range(2):
            x_copy(k, ch).wait_send()
            for way in range(2):
                row_copy(k, way, ch).wait_send()


def write_out(w, s, out_w, out_s, sem):
    copies = [
        pltpu.make_async_copy(w.at[pl.ds(a, n)], out_w.at[pl.ds(c, n)], sem.at[i])
        for i, (a, n, c) in enumerate(NATURAL)
    ]
    copies.append(pltpu.make_async_copy(s, out_s, sem.at[4]))
    for c in copies:
        c.start()
    for c in copies:
        c.wait()


def solution(mesh):
    n_dom = mesh.shape["dom"]

    def body(embedding, adagrad_state, relation_table, source_row, target_row, relation_id, negative_row):
        vmem = pl.BlockSpec(memory_space=pltpu.VMEM)
        hbm = pl.BlockSpec(memory_space=pltpu.HBM)
        dma = pltpu.SemaphoreType.DMA
        new_w, new_s = pl.pallas_call(
            functools.partial(kernel, n_dom),
            out_shape=(pltpu.VMEM((COLS, ROWS), F32), pltpu.VMEM((1, ROWS), F32)),
            in_specs=[hbm] * 7,
            out_specs=(vmem, vmem),
            scratch_shapes=[
                pltpu.VMEM((COLS, ROWS), F32),
                pltpu.VMEM((1, ROWS), F32),
                pltpu.VMEM((COLS, 128), BF16),
                pltpu.VMEM(source_row.shape, jnp.int32),
                pltpu.VMEM(target_row.shape, jnp.int32),
                pltpu.VMEM(relation_id.shape, jnp.int32),
                pltpu.VMEM(negative_row.shape, jnp.int32),
                pltpu.VMEM((2, 8, E), jnp.int32),
                pltpu.VMEM((2, GROUPS, 8, E), jnp.int32),
                pltpu.VMEM((2, 2, COLS, ROWS), BF16),
                pltpu.VMEM((ROWS, 2 * CHUNKS[0][1]), BF16),
                pltpu.VMEM((ROWS, 2 * CHUNKS[1][1]), BF16),
                pltpu.VMEM((COLS, GROUPS * E), BF16),
                pltpu.VMEM((COLS, GROUPS * E), BF16),
                pltpu.VMEM((ROWS, GROUPS * E), F32),
                pltpu.VMEM((ROWS, GROUPS * E), BF16),
                pltpu.VMEM((ROWS, GROUPS), F32),
                pltpu.VMEM((ROWS, GROUPS * E), BF16),
                pltpu.VMEM((COLS, GROUPS * E), BF16),
                pltpu.VMEM((2, COLS, ROWS), BF16),
                pltpu.VMEM((2, COLS, ROWS), BF16),
                dma((5,)),
                dma((2, 4)),
                dma((4,)),
                dma((2, 2, 2)),
                dma((2, 2, 2)),
                dma((2, 4)),
                dma((2, 4)),
                dma((2, 2)),
                dma((2, 2)),
            ],
            compiler_params=pltpu.CompilerParams(
                collective_id=0, has_side_effects=True, vmem_limit_bytes=32 * 2**20
            ),
        )(
            *(
                pltpu.with_memory_space_constraint(x, pltpu.HBM)
                for x in (
                    embedding.T,
                    adagrad_state.reshape(1, ROWS),
                    relation_table.T,
                    source_row,
                    target_row,
                    relation_id,
                    negative_row,
                )
            )
        )
        new_w, new_s = pl.pallas_call(
            write_out,
            out_shape=(pltpu.HBM((COLS, ROWS), F32), pltpu.HBM((1, ROWS), F32)),
            in_specs=[vmem, vmem],
            out_specs=(hbm, hbm),
            scratch_shapes=[dma((5,))],
        )(*(pltpu.with_memory_space_constraint(x, pltpu.VMEM) for x in (new_w, new_s)))
        return new_w.T, new_s.reshape(ROWS)

    in_specs = (
        P("dom", None),
        P("dom"),
        P(),
        P(None, "dom", "edge"),
        P(None, "dom", "edge"),
        P(None, "dom", "edge"),
        P(None, "dom", "edge", None),
    )
    out_specs = (P("dom", None), P("dom"))
    return jax.shard_map(body, mesh=mesh, in_specs=in_specs, out_specs=out_specs, check_vma=False)
```

```python
import functools

import jax
import jax.numpy as jnp
from jax import lax
from jax.experimental import pallas as pl
from jax.experimental.pallas import tpu as pltpu
from jax.sharding import PartitionSpec as P

MESH = pl.DeviceIdType.MESH
F32 = jnp.float32
BF16 = jnp.bfloat16

learning_rate = 0.1
ROWS = 256
HALF = 128
GROUPS = 4
E = 256
COLS = 800

CHUNKS = ((0, 128, 0), (256, 128, 128), (512, 144, 256))
N_CH = len(CHUNKS)
ACROSS = 0
SPANS = ((0, 2), (2, 3))
NATURAL = [(a, n, c) for a, n, c in CHUNKS] + [(a + n, n, c + 400) for a, n, c in CHUNKS]


def chunk(ch):
    a, n, _ = CHUNKS[ch]
    return pl.ds(a, 2 * n)


def parts(ch):
    a, n, _ = CHUNKS[ch]
    return pl.ds(a, n), pl.ds(a + n, n)


def span(j):
    first, last = CHUNKS[SPANS[j][0]], CHUNKS[SPANS[j][1] - 1]
    return pl.ds(first[0], last[0] + 2 * last[1] - first[0])


def dot(a, b, ca, cb):
    return lax.dot_general(a, b, (((ca,), (cb,)), ((), ())), preferred_element_type=F32)


def kernel(
    n_dom,
    emb, state, rel, src, tgt, rid, neg,
    out_w, out_s,
    w, statev, relv, srcv, tgtv, ridv, negv,
    pack, sib_pack, idx, buf, bt, r, q, part, ots, lc, gt, gs, xs, xr,
    load_sem, emb_sem, rel_sem, row_send, row_recv, idx_send, idx_recv, x_send, x_recv, relay,
):
    d = lax.axis_index("dom")
    e = lax.axis_index("edge")
    core = lax.rem(e, 2)
    plane = e - core
    sibling = plane + (1 - core)
    up = [lax.rem(d + k + 1, n_dom) for k in range(2)]
    down = [lax.rem(d + n_dom - k - 1, n_dom) for k in range(2)]
    mine = pl.ds(pl.multiple_of(core * HALF, HALF), HALF)
    other = pl.ds(pl.multiple_of((1 - core) * HALF, HALF), HALF)

    index_loads = [
        pltpu.make_async_copy(a, b, load_sem.at[i])
        for i, (a, b) in enumerate(((src, srcv), (tgt, tgtv), (rid, ridv), (neg, negv), (state, statev)))
    ]
    emb_loads = [
        pltpu.make_async_copy(emb.at[pl.ds(c, n), half], w.at[pl.ds(a, n), half], emb_sem.at[j, i])
        for j, half in enumerate((mine, other))
        for i, (a, n, c) in enumerate(NATURAL)
    ]
    rel_loads = [
        pltpu.make_async_copy(rel.at[pl.ds(c, n)], relv.at[pl.ds(a, n)], rel_sem.at[i])
        for i, (a, n, c) in enumerate(NATURAL)
    ]
    for c in index_loads[:4] + emb_loads[: 2 * N_CH]:
        c.start()

    barrier = pltpu.get_barrier_semaphore()

    def tell(dom, edge):
        pl.semaphore_signal(barrier, inc=1, device_id=(dom, edge), device_id_type=MESH)

    @pl.when(core == 0)
    def _():
        tell(down[0], plane)
        tell(d, 3 - plane)

    @pl.when(core == 1)
    def _():
        tell(d, plane)
        tell(up[0], plane)
        tell(up[0], 3 - plane)

    for c in index_loads[:4]:
        c.wait()
    for k in range(2):
        pack[k, 0:1, :] = srcv[k]
        pack[k, 1:2, :] = tgtv[k]
        pack[k, 2:3, :] = ridv[k]
        for j in range(4):
            pack[k, 3 + j : 4 + j, :] = negv[k, 0, :, 256 * j : 256 * (j + 1)]

    order = [lax.rem(plane + o, GROUPS) for o in range(GROUPS)]

    def pass_on(j, dom, edge):
        pl.semaphore_signal(relay.at[j], inc=1, device_id=(dom, edge), device_id_type=MESH)

    @pl.when(core == 0)
    def _():
        pl.semaphore_wait(barrier, 3)
        pass_on(2, d, sibling)
        pass_on(0, up[0], plane)
        pass_on(0, down[0], plane + 1)

    @pl.when(core == 1)
    def _():
        pl.semaphore_wait(relay.at[2], 1)

    def idx_copy(j, source, target, recv, dom, edge):
        return pltpu.make_async_remote_copy(
            src_ref=source,
            dst_ref=target,
            send_sem=idx_send.at[j],
            recv_sem=idx_recv.at[recv],
            device_id=(dom, edge),
            device_id_type=MESH,
        )

    to_sibling = idx_copy(0, pack, sib_pack, 5, d, sibling)
    to_own = idx_copy(0, pack, idx.at[:, e], e, d, plane)
    to_down = idx_copy(1, pack.at[0], idx.at[0, e], e, down[0], plane + 1)
    to_down2 = idx_copy(2, idx.at[1], idx.at[1], 4, down[1], plane + 1)
    across = [
        idx_copy(2, pack, idx.at[:, e], e, d, 2 - plane),
        idx_copy(3, sib_pack, idx.at[:, e - core], e - core, d, 2 - plane),
        idx_copy(4, pack.at[0], idx.at[0, e], e, down[0], 3 - plane),
        idx_copy(5, sib_pack.at[0], idx.at[0, e - core], e - core, down[0], 3 - plane),
    ]

    def idx_wait(k, g):
        @pl.when(core == 0)
        def _():
            if k == 0:
                pl.when(e != g)(lambda: idx_copy(0, pack, idx.at[:, g], g, d, sibling).wait_recv())

        @pl.when(core == 1)
        def _():
            if k == 0:
                idx_copy(1, pack.at[0], idx.at[0, g], g, d, sibling).wait_recv()
            else:
                pl.when(g == order[0])(to_down2.wait_recv)

    def row_copy(k, way, ch):
        return pltpu.make_async_remote_copy(
            src_ref=buf.at[k, core, core, chunk(ch)],
            dst_ref=buf.at[k, 1 - way, core, chunk(ch)],
            send_sem=row_send.at[k, way, ch],
            recv_sem=row_recv.at[k, core, ch],
            device_id=((up[k], plane), (down[k], plane + 1))[way],
            device_id_type=MESH,
        )

    def row_arrival(k, half, ch):
        return pltpu.make_async_remote_copy(
            src_ref=buf.at[k, core, half, chunk(ch)],
            dst_ref=buf.at[k, 1 - core, half, chunk(ch)],
            send_sem=row_send.at[k, half, ch],
            recv_sem=row_recv.at[k, half, ch],
            device_id=(d, sibling),
            device_id_type=MESH,
        )

    def x_copy(k, j):
        return pltpu.make_async_remote_copy(
            src_ref=xs.at[k, span(j)],
            dst_ref=xr.at[k, span(j)],
            send_sem=x_send.at[k, j],
            recv_sem=x_recv.at[k, j],
            device_id=(d, sibling),
            device_id_type=MESH,
        )

    pl.when(core == 0)(to_sibling.start)
    pl.when(core == 1)(to_own.start)
    to_down.start()
    for ch in range(N_CH):
        emb_loads[ch].wait()
        emb_loads[N_CH + ch].wait()
        buf[0, core, core, chunk(ch)] = w[chunk(ch), mine].astype(BF16)
        for way in range(2):
            row_copy(0, way, ch).start()
        if ch == ACROSS:

            @pl.when(core == 1)
            def _():
                to_sibling.wait_recv()
                pl.semaphore_wait(barrier, 2)
                for c in across:
                    c.start()

    for c in emb_loads[2 * N_CH :] + rel_loads + index_loads[4:]:
        c.start()

    @pl.when(core == 0)
    def _():
        for k in range(2):
            idx[k, e] = pack[k]

    for c in emb_loads[2 * N_CH :]:
        c.wait()
    buf[0, core, 1 - core] = w[:, other].astype(BF16)
    for c in rel_loads + index_loads[4:]:
        c.wait()

    def prepare(k, g):
        idx_wait(k, g)
        cols = pl.ds(pl.multiple_of(g * E, E), E)
        at = lax.broadcasted_iota(jnp.int32, (ROWS, E), 0)
        ots[:, cols] = jnp.where(at == idx[k, g, 0:1, :], 1.0, 0.0).astype(BF16)
        count = jnp.zeros((ROWS, E), F32)
        for j in range(4):
            count += jnp.where(at == idx[k, g, 3 + j : 4 + j, :], 1.0, 0.0)
        lc[g] = jnp.log(jnp.sum(count, axis=1, keepdims=True))
        kind = jnp.where(at[:HALF] == idx[k, g, 2:3, :], 1.0, 0.0).astype(BF16)
        r[:, cols] = dot(relv[...], kind, 1, 0).astype(BF16)

    def whole(k, slot, ch):
        return jnp.concatenate([buf[k, slot, half, chunk(ch)] for half in range(2)], axis=1)

    def flip(k, ch):
        for half in range(2):
            bt[half * HALF : (half + 1) * HALF, chunk(ch)] = buf[k, 1, half, chunk(ch)].T

    def products(k, ch, g):
        re, im = parts(ch)
        n = CHUNKS[ch][1]
        cols = pl.ds(pl.multiple_of(g * E, E), E)
        s = dot(whole(k, 0, ch), ots[:, cols], 1, 0)
        rr = r[re, cols].astype(F32)
        ri = r[im, cols].astype(F32)
        q[re, cols] = (s[:n] * rr - s[n:] * ri).astype(BF16)
        q[im, cols] = (s[:n] * ri + s[n:] * rr).astype(BF16)

    def scores(ch):
        for g in range(GROUPS):
            cols = slice(g * E, (g + 1) * E)
            new = dot(bt[:, chunk(ch)], q[chunk(ch), cols], 1, 0)
            part[:, cols] = new if ch == 0 else part[:, cols] + new

    def pulls(k):
        at = lax.broadcasted_iota(jnp.int32, (ROWS, E), 0)
        for g in range(GROUPS):
            cols = slice(g * E, (g + 1) * E)
            score = part[:, cols] + dot(bt[:, chunk(N_CH - 1)], q[chunk(N_CH - 1), cols], 1, 0)
            hit = at == idx[k, g, 1:2, :]
            pos = jnp.sum(jnp.where(hit, score, 0.0), axis=0, keepdims=True)
            z = score + lc[g]
            top = jnp.maximum(jnp.max(z, axis=0, keepdims=True), pos)
            ez = jnp.exp(z - top)
            ep = jnp.exp(pos - top)
            inv = 1.0 / (jnp.sum(ez, axis=0, keepdims=True) + ep)
            pull = ep * inv - 1.0
            gt[:, cols] = (ez * inv + jnp.where(hit, pull, 0.0)).astype(BF16)

    def source_terms(k, ch):
        re, im = parts(ch)
        n = CHUNKS[ch][1]
        for g in range(GROUPS):
            cols = slice(g * E, (g + 1) * E)
            gq = dot(whole(k, 1, ch), gt[:, cols], 1, 0).astype(BF16)
            rr, ri = r[re, cols], r[im, cols]
            gs[re, cols] = gq[:n] * rr + gq[n:] * ri
            gs[im, cols] = gq[n:] * rr - gq[:n] * ri

    def update(k, half, lane):
        g = xs[k, :, lane].astype(F32) + xr[k, :, lane].astype(F32)
        new_s = statev[:, lane] + jnp.sum(g * g, axis=0, keepdims=True) * (1.0 / COLS)
        new_w = w[:, lane] - g * (learning_rate * lax.rsqrt(new_s))
        if k == 0:
            statev[:, lane] = new_s
            w[:, lane] = new_w
            buf[1, core, half] = new_w.astype(BF16)
        else:
            out_s[:, lane] = new_s
            out_w[:, lane] = new_w

    for k in range(2):
        for o in range(GROUPS):
            prepare(k, order[o])

            @pl.when(core == 0)
            def _():
                for ch in range(N_CH):
                    products(k, ch, order[o])

        @pl.when(core == 1)
        def _():
            for ch in range(N_CH):
                flip(k, ch)

        for ch in range(N_CH):
            for half in range(2):
                row_arrival(k, half, ch).wait_recv()
            pl.when(core == 0)(lambda: flip(k, ch))

            @pl.when(core == 1)
            def _():
                for g in range(GROUPS):
                    products(k, ch, g)

            if ch < N_CH - 1:
                scores(ch)
        pulls(k)
        for j in range(2):

            @pl.when(core == 0)
            def _():
                for ch in range(*SPANS[j]):
                    source_terms(k, ch)
                xs[k, span(j)] = dot(gs[span(j), :], ots[...], 1, 1).astype(BF16)

            @pl.when(core == 1)
            def _():
                xs[k, span(j)] = dot(q[span(j), :], gt[...], 1, 1).astype(BF16)

            x_copy(k, j).start()
        if k == 0:
            pl.semaphore_wait(relay.at[0], 1)
            pass_on(1, d, sibling)
        for j in range(2):
            x_copy(k, j).wait_recv()
        update(k, core, mine)
        if k == 0:
            pl.semaphore_wait(relay.at[1], 1)
            pl.when(core == 0)(to_down2.start)
            for ch in range(N_CH):
                for way in range(2):
                    row_copy(1, way, ch).start()
        update(k, 1 - core, other)

    to_down.wait_send()

    @pl.when(core == 0)
    def _():
        to_sibling.wait_send()
        to_down2.wait_send()

    @pl.when(core == 1)
    def _():
        for c in [to_own] + across:
            c.wait_send()

    for k in range(2):
        for j in range(2):
            x_copy(k, j).wait_send()
        for ch in range(N_CH):
            for way in range(2):
                row_copy(k, way, ch).wait_send()


def write_out(w, s, out_w, out_s, sem):
    copies = [
        pltpu.make_async_copy(w.at[pl.ds(a, n)], out_w.at[pl.ds(c, n)], sem.at[i])
        for i, (a, n, c) in enumerate(NATURAL)
    ]
    copies.append(pltpu.make_async_copy(s, out_s, sem.at[2 * N_CH]))
    for c in copies:
        c.start()
    for c in copies:
        c.wait()


def solution(mesh):
    n_dom = mesh.shape["dom"]

    def body(embedding, adagrad_state, relation_table, source_row, target_row, relation_id, negative_row):
        vmem = pl.BlockSpec(memory_space=pltpu.VMEM)
        hbm = pl.BlockSpec(memory_space=pltpu.HBM)
        dma = pltpu.SemaphoreType.DMA
        new_w, new_s = pl.pallas_call(
            functools.partial(kernel, n_dom),
            out_shape=(pltpu.VMEM((COLS, ROWS), F32), pltpu.VMEM((1, ROWS), F32)),
            in_specs=[hbm] * 7,
            out_specs=(vmem, vmem),
            scratch_shapes=[
                pltpu.VMEM((COLS, ROWS), F32),
                pltpu.VMEM((1, ROWS), F32),
                pltpu.VMEM((COLS, 128), BF16),
                pltpu.VMEM(source_row.shape, jnp.int32),
                pltpu.VMEM(target_row.shape, jnp.int32),
                pltpu.VMEM(relation_id.shape, jnp.int32),
                pltpu.VMEM(negative_row.shape, jnp.int32),
                pltpu.VMEM((2, 8, E), jnp.int32),
                pltpu.VMEM((2, 8, E), jnp.int32),
                pltpu.VMEM((2, GROUPS, 8, E), jnp.int32),
                pltpu.VMEM((2, 2, 2, COLS, HALF), BF16),
                pltpu.VMEM((ROWS, COLS), BF16),
                pltpu.VMEM((COLS, GROUPS * E), BF16),
                pltpu.VMEM((COLS, GROUPS * E), BF16),
                pltpu.VMEM((ROWS, GROUPS * E), F32),
                pltpu.VMEM((ROWS, GROUPS * E), BF16),
                pltpu.VMEM((GROUPS, ROWS, 1), F32),
                pltpu.VMEM((ROWS, GROUPS * E), BF16),
                pltpu.VMEM((COLS, GROUPS * E), BF16),
                pltpu.VMEM((2, COLS, ROWS), BF16),
                pltpu.VMEM((2, COLS, ROWS), BF16),
                dma((5,)),
                dma((2, 2 * N_CH)),
                dma((2 * N_CH,)),
                dma((2, 2, N_CH)),
                dma((2, 2, N_CH)),
                dma((6,)),
                dma((6,)),
                dma((2, 2)),
                dma((2, 2)),
                pltpu.SemaphoreType.REGULAR((3,)),
            ],
            compiler_params=pltpu.CompilerParams(
                collective_id=0, has_side_effects=True, vmem_limit_bytes=32 * 2**20
            ),
        )(
            *(
                pltpu.with_memory_space_constraint(x, pltpu.HBM)
                for x in (
                    embedding.T,
                    adagrad_state.reshape(1, ROWS),
                    relation_table.T,
                    source_row,
                    target_row,
                    relation_id,
                    negative_row,
                )
            )
        )
        new_w, new_s = pl.pallas_call(
            write_out,
            out_shape=(pltpu.HBM((COLS, ROWS), F32), pltpu.HBM((1, ROWS), F32)),
            in_specs=[vmem, vmem],
            out_specs=(hbm, hbm),
            scratch_shapes=[dma((2 * N_CH + 1,))],
        )(*(pltpu.with_memory_space_constraint(x, pltpu.VMEM) for x in (new_w, new_s)))
        return new_w.T, new_s.reshape(ROWS)

    in_specs = (
        P("dom", None),
        P("dom"),
        P(),
        P(None, "dom", "edge"),
        P(None, "dom", "edge"),
        P(None, "dom", "edge"),
        P(None, "dom", "edge", None),
    )
    out_specs = (P("dom", None), P("dom"))
    return jax.shard_map(body, mesh=mesh, in_specs=in_specs, out_specs=out_specs, check_vma=False)
```

```python
import functools

import jax
import jax.numpy as jnp
from jax import lax
from jax.experimental import pallas as pl
from jax.experimental.pallas import tpu as pltpu
from jax.sharding import PartitionSpec as P

MESH = pl.DeviceIdType.MESH
F32 = jnp.float32
BF16 = jnp.bfloat16

learning_rate = 0.1
ROWS = 256
HALF = 128
GROUPS = 4
E = 256
COLS = 800

CHUNKS = ((0, 192, 0), (384, 128, 192), (640, 80, 320))
N_CH = len(CHUNKS)
RING = 8
SPANS = ((0, 2), (2, 3))
NATURAL = [(a, n, c) for a, n, c in CHUNKS] + [(a + n, n, c + 400) for a, n, c in CHUNKS]


def chunk(ch):
    a, n, _ = CHUNKS[ch]
    return pl.ds(a, 2 * n)


def parts(ch):
    a, n, _ = CHUNKS[ch]
    return pl.ds(a, n), pl.ds(a + n, n)


def span(j):
    first, last = CHUNKS[SPANS[j][0]], CHUNKS[SPANS[j][1] - 1]
    return pl.ds(first[0], last[0] + 2 * last[1] - first[0])


def dot(a, b, ca, cb):
    return lax.dot_general(a, b, (((ca,), (cb,)), ((), ())), preferred_element_type=F32)


def kernel(
    n_dom,
    emb, state, rel, src, tgt, rid, neg,
    out_w, out_s,
    w, statev, relv, srcv, tgtv, ridv, negv,
    pack, idx, buf, bt, r, q, part, ots, lc, gt, gs, xs, xr,
    load_sem, emb_sem, rel_sem, row_send, row_recv, idx_send, idx_recv, x_send, x_recv, relay,
):
    d = lax.axis_index("dom")
    e = lax.axis_index("edge")
    core = lax.rem(e, 2)
    plane = e - core
    sibling = plane + (1 - core)
    up = [lax.rem(d + k + 1, n_dom) for k in range(2)]
    down = [lax.rem(d + n_dom - k - 1, n_dom) for k in range(2)]
    mine = pl.ds(pl.multiple_of(core * HALF, HALF), HALF)
    other = pl.ds(pl.multiple_of((1 - core) * HALF, HALF), HALF)

    barrier = pltpu.get_barrier_semaphore()

    def tell(dom, edge):
        pl.semaphore_signal(barrier, inc=1, device_id=(dom, edge), device_id_type=MESH)

    @pl.when(core == 0)
    def _():
        tell(down[0], plane)
        tell(d, sibling)
        tell(d, 3 - plane)

    first = lax.rem(d, RING) == 0
    last = lax.rem(d, RING) == RING - 1

    @pl.when(core == 1)
    def _():
        tell(up[0], plane)
        tell(d, plane)
        pl.when(jnp.logical_not(last))(lambda: tell(up[0], 3 - plane))

    index_loads = [
        pltpu.make_async_copy(a, b, load_sem.at[i])
        for i, (a, b) in enumerate(((src, srcv), (tgt, tgtv), (rid, ridv), (neg, negv), (state, statev)))
    ]
    emb_loads = [
        pltpu.make_async_copy(emb.at[pl.ds(c, n), half], w.at[pl.ds(a, n), half], emb_sem.at[j, i])
        for j, half in enumerate((mine, other))
        for i, (a, n, c) in enumerate(NATURAL)
    ]
    rel_loads = [
        pltpu.make_async_copy(rel.at[pl.ds(c, n)], relv.at[pl.ds(a, n)], rel_sem.at[i])
        for i, (a, n, c) in enumerate(NATURAL)
    ]
    for c in index_loads[:4] + emb_loads[: 2 * N_CH]:
        c.start()

    for c in index_loads[:4]:
        c.wait()
    for k in range(2):
        pack[k, 0:1, :] = srcv[k]
        pack[k, 1:2, :] = tgtv[k]
        pack[k, 2:3, :] = ridv[k]
        for j in range(4):
            pack[k, 3 + j : 4 + j, :] = negv[k, 0, :, 256 * j : 256 * (j + 1)]

    order = [lax.rem(plane + o, GROUPS) for o in range(GROUPS)]

    def pass_on(j, dom, edge):
        pl.semaphore_signal(relay.at[j], inc=1, device_id=(dom, edge), device_id_type=MESH)

    for ch in range(N_CH):
        emb_loads[ch].wait()
        emb_loads[N_CH + ch].wait()
        buf[0, core, core, chunk(ch)] = w[chunk(ch), mine].astype(BF16)

    def idx_copy(j, source, target, recv, dom, edge):
        return pltpu.make_async_remote_copy(
            src_ref=source,
            dst_ref=target,
            send_sem=idx_send.at[j],
            recv_sem=idx_recv.at[recv],
            device_id=(dom, edge),
            device_id_type=MESH,
        )

    to_own = idx_copy(0, pack, idx.at[:, e], e, d, plane)
    to_down = idx_copy(1, pack.at[0], idx.at[0, e], e, down[0], plane + 1)
    to_down2 = idx_copy(2, idx.at[1], idx.at[1], 4, down[1], plane + 1)
    across = idx_copy(4, pack, idx.at[:, e], e, d, 2 - plane)
    down_across = idx_copy(3, pack.at[0], idx.at[0, e], e, down[0], 3 - plane)
    both = pl.ds(2 - plane, 2)
    onward = idx_copy(0, idx.at[0, both], idx.at[0, both], 2 - plane, down[0], plane + 1)

    def cross(heard):
        @pl.when(core == 1)
        def _():
            pl.semaphore_wait(barrier, heard)
            pass_on(3, d, sibling)

        pl.when(core == 0)(lambda: pl.semaphore_wait(relay.at[3], 1))
        across.start()

    @pl.when(first)
    def _():
        cross(2)
        pl.when(core == 1)(to_own.start)

    @pl.when(core == 0)
    def _():
        pl.semaphore_wait(barrier, 3)
        pass_on(2, d, sibling)
        pass_on(0, up[0], plane)
        pass_on(0, down[0], plane + 1)

    @pl.when(core == 1)
    def _():
        pl.semaphore_wait(relay.at[2], 1)

    def send_onward():
        for h in (2, 3):
            idx_copy(0, pack, idx.at[:, order[h]], order[h], d, sibling).wait_recv()
        onward.start()

    def idx_wait(k, o):
        g = order[o]

        @pl.when(core == 0)
        def _():
            if k == 0 and o < 2:
                pl.when(e != g)(lambda: idx_copy(0, pack, idx.at[:, g], g, d, sibling).wait_recv())
            elif k == 0 and o == 2:

                @pl.when(jnp.logical_not(first))
                def _():
                    for h in (2, 3):
                        idx_copy(0, pack, idx.at[:, order[h]], order[h], d, sibling).wait_recv()

        @pl.when(core == 1)
        def _():
            if k == 0 and o < 2:
                idx_copy(1, pack.at[0], idx.at[0, g], g, d, sibling).wait_recv()
            elif k == 0 and o == 2:
                pl.when(last)(onward.wait_recv)

                @pl.when(jnp.logical_not(last))
                def _():
                    for h in (2, 3):
                        idx_copy(1, pack.at[0], idx.at[0, order[h]], order[h], d, sibling).wait_recv()
            elif k == 1 and o == 0:
                to_down2.wait_recv()

    def row_copy(k, way, ch):
        return pltpu.make_async_remote_copy(
            src_ref=buf.at[k, core, core, chunk(ch)],
            dst_ref=buf.at[k, 1 - way, core, chunk(ch)],
            send_sem=row_send.at[k, way, ch],
            recv_sem=row_recv.at[k, core, ch],
            device_id=((up[k], plane), (down[k], plane + 1))[way],
            device_id_type=MESH,
        )

    def row_arrival(k, half, ch):
        return pltpu.make_async_remote_copy(
            src_ref=buf.at[k, core, half, chunk(ch)],
            dst_ref=buf.at[k, 1 - core, half, chunk(ch)],
            send_sem=row_send.at[k, half, ch],
            recv_sem=row_recv.at[k, half, ch],
            device_id=(d, sibling),
            device_id_type=MESH,
        )

    def x_copy(k, j):
        return pltpu.make_async_remote_copy(
            src_ref=xs.at[k, span(j)],
            dst_ref=xr.at[k, span(j)],
            send_sem=x_send.at[k, j],
            recv_sem=x_recv.at[k, j],
            device_id=(d, sibling),
            device_id_type=MESH,
        )

    pl.when(jnp.logical_and(core == 1, jnp.logical_not(first)))(to_own.start)
    to_down.start()
    pl.when(jnp.logical_and(core == 0, first))(send_onward)
    for ch in range(N_CH):
        for way in (1, 0):
            row_copy(0, way, ch).start()
        if ch == 0:

            @pl.when(jnp.logical_not(first))
            def _():
                cross(3)
                down_across.start()

    for c in emb_loads[2 * N_CH :] + rel_loads + index_loads[4:]:
        c.start()

    @pl.when(core == 0)
    def _():
        for k in range(2):
            idx[k, e] = pack[k]

    for c in emb_loads[2 * N_CH :]:
        c.wait()
    buf[0, core, 1 - core] = w[:, other].astype(BF16)
    for c in rel_loads + index_loads[4:]:
        c.wait()

    def prepare(k, o):
        idx_wait(k, o)
        g = order[o]
        cols = pl.ds(pl.multiple_of(g * E, E), E)
        at = lax.broadcasted_iota(jnp.int32, (ROWS, E), 0)
        ots[:, cols] = jnp.where(at == idx[k, g, 0:1, :], 1.0, 0.0).astype(BF16)
        count = jnp.zeros((ROWS, E), F32)
        for j in range(4):
            count += jnp.where(at == idx[k, g, 3 + j : 4 + j, :], 1.0, 0.0)
        lc[g] = jnp.log(jnp.sum(count, axis=1, keepdims=True))
        kind = jnp.where(at[:HALF] == idx[k, g, 2:3, :], 1.0, 0.0).astype(BF16)
        r[:, cols] = dot(relv[...], kind, 1, 0).astype(BF16)

    def whole(k, slot, ch):
        return jnp.concatenate([buf[k, slot, half, chunk(ch)] for half in range(2)], axis=1)

    def flip(k, ch):
        for half in range(2):
            bt[half * HALF : (half + 1) * HALF, chunk(ch)] = buf[k, 1, half, chunk(ch)].T

    def products(k, ch, g):
        re, im = parts(ch)
        n = CHUNKS[ch][1]
        cols = pl.ds(pl.multiple_of(g * E, E), E)
        s = dot(whole(k, 0, ch), ots[:, cols], 1, 0)
        rr = r[re, cols].astype(F32)
        ri = r[im, cols].astype(F32)
        q[re, cols] = (s[:n] * rr - s[n:] * ri).astype(BF16)
        q[im, cols] = (s[:n] * ri + s[n:] * rr).astype(BF16)

    def scores(ch):
        for g in range(GROUPS):
            cols = slice(g * E, (g + 1) * E)
            new = dot(bt[:, chunk(ch)], q[chunk(ch), cols], 1, 0)
            part[:, cols] = new if ch == 0 else part[:, cols] + new

    def pulls(k):
        at = lax.broadcasted_iota(jnp.int32, (ROWS, E), 0)
        for g in range(GROUPS):
            cols = slice(g * E, (g + 1) * E)
            score = part[:, cols] + dot(bt[:, chunk(N_CH - 1)], q[chunk(N_CH - 1), cols], 1, 0)
            hit = at == idx[k, g, 1:2, :]
            pos = jnp.sum(jnp.where(hit, score, 0.0), axis=0, keepdims=True)
            z = score + lc[g]
            top = jnp.maximum(jnp.max(z, axis=0, keepdims=True), pos)
            ez = jnp.exp(z - top)
            ep = jnp.exp(pos - top)
            inv = 1.0 / (jnp.sum(ez, axis=0, keepdims=True) + ep)
            pull = ep * inv - 1.0
            gt[:, cols] = (ez * inv + jnp.where(hit, pull, 0.0)).astype(BF16)

    def source_terms(k, ch):
        re, im = parts(ch)
        n = CHUNKS[ch][1]
        for g in range(GROUPS):
            cols = slice(g * E, (g + 1) * E)
            gq = dot(whole(k, 1, ch), gt[:, cols], 1, 0).astype(BF16)
            rr, ri = r[re, cols], r[im, cols]
            gs[re, cols] = gq[:n] * rr + gq[n:] * ri
            gs[im, cols] = gq[n:] * rr - gq[:n] * ri

    def update(k, half, lane):
        g = xs[k, :, lane].astype(F32) + xr[k, :, lane].astype(F32)
        new_s = statev[:, lane] + jnp.sum(g * g, axis=0, keepdims=True) * (1.0 / COLS)
        new_w = w[:, lane] - g * (learning_rate * lax.rsqrt(new_s))
        if k == 0:
            statev[:, lane] = new_s
            w[:, lane] = new_w
            buf[1, core, half] = new_w.astype(BF16)
        else:
            out_s[:, lane] = new_s
            out_w[:, lane] = new_w

    for k in range(2):
        for o in range(GROUPS):
            prepare(k, o)

            @pl.when(core == 0)
            def _():
                for ch in range(N_CH):
                    products(k, ch, order[o])

        @pl.when(core == 1)
        def _():
            for ch in range(N_CH):
                flip(k, ch)

        for ch in range(N_CH):
            for half in range(2):
                row_arrival(k, half, ch).wait_recv()
            pl.when(core == 0)(lambda: flip(k, ch))

            @pl.when(core == 1)
            def _():
                for g in range(GROUPS):
                    products(k, ch, g)

            if ch < N_CH - 1:
                scores(ch)
        if k == 0:
            pl.semaphore_wait(relay.at[0], 1)
            pass_on(1, d, sibling)
            pl.when(core == 0)(to_down2.start)
        pulls(k)
        for j in range(2):

            @pl.when(core == 0)
            def _():
                for ch in range(*SPANS[j]):
                    source_terms(k, ch)
                xs[k, span(j)] = dot(gs[span(j), :], ots[...], 1, 1).astype(BF16)

            @pl.when(core == 1)
            def _():
                xs[k, span(j)] = dot(q[span(j), :], gt[...], 1, 1).astype(BF16)

            x_copy(k, j).start()
        for j in range(2):
            x_copy(k, j).wait_recv()
        update(k, core, mine)
        if k == 0:
            pl.semaphore_wait(relay.at[1], 1)
            for ch in range(N_CH):
                for way in range(2):
                    row_copy(1, way, ch).start()
        update(k, 1 - core, other)

    to_down.wait_send()
    across.wait_send()
    pl.when(jnp.logical_not(first))(down_across.wait_send)

    @pl.when(core == 0)
    def _():
        to_down2.wait_send()
        pl.when(first)(onward.wait_send)

    @pl.when(core == 1)
    def _():
        to_own.wait_send()

    for k in range(2):
        for j in range(2):
            x_copy(k, j).wait_send()
        for ch in range(N_CH):
            for way in range(2):
                row_copy(k, way, ch).wait_send()


def write_out(w, s, out_w, out_s, sem):
    copies = [
        pltpu.make_async_copy(w.at[pl.ds(a, n)], out_w.at[pl.ds(c, n)], sem.at[i])
        for i, (a, n, c) in enumerate(NATURAL)
    ]
    copies.append(pltpu.make_async_copy(s, out_s, sem.at[2 * N_CH]))
    for c in copies:
        c.start()
    for c in copies:
        c.wait()


def solution(mesh):
    n_dom = mesh.shape["dom"]

    def body(embedding, adagrad_state, relation_table, source_row, target_row, relation_id, negative_row):
        vmem = pl.BlockSpec(memory_space=pltpu.VMEM)
        hbm = pl.BlockSpec(memory_space=pltpu.HBM)
        dma = pltpu.SemaphoreType.DMA
        new_w, new_s = pl.pallas_call(
            functools.partial(kernel, n_dom),
            out_shape=(pltpu.VMEM((COLS, ROWS), F32), pltpu.VMEM((1, ROWS), F32)),
            in_specs=[hbm] * 7,
            out_specs=(vmem, vmem),
            scratch_shapes=[
                pltpu.VMEM((COLS, ROWS), F32),
                pltpu.VMEM((1, ROWS), F32),
                pltpu.VMEM((COLS, 128), BF16),
                pltpu.VMEM(source_row.shape, jnp.int32),
                pltpu.VMEM(target_row.shape, jnp.int32),
                pltpu.VMEM(relation_id.shape, jnp.int32),
                pltpu.VMEM(negative_row.shape, jnp.int32),
                pltpu.VMEM((2, 8, E), jnp.int32),
                pltpu.VMEM((2, GROUPS, 8, E), jnp.int32),
                pltpu.VMEM((2, 2, 2, COLS, HALF), BF16),
                pltpu.VMEM((ROWS, COLS), BF16),
                pltpu.VMEM((COLS, GROUPS * E), BF16),
                pltpu.VMEM((COLS, GROUPS * E), BF16),
                pltpu.VMEM((ROWS, GROUPS * E), F32),
                pltpu.VMEM((ROWS, GROUPS * E), BF16),
                pltpu.VMEM((GROUPS, ROWS, 1), F32),
                pltpu.VMEM((ROWS, GROUPS * E), BF16),
                pltpu.VMEM((COLS, GROUPS * E), BF16),
                pltpu.VMEM((2, COLS, ROWS), BF16),
                pltpu.VMEM((2, COLS, ROWS), BF16),
                dma((5,)),
                dma((2, 2 * N_CH)),
                dma((2 * N_CH,)),
                dma((2, 2, N_CH)),
                dma((2, 2, N_CH)),
                dma((5,)),
                dma((5,)),
                dma((2, 2)),
                dma((2, 2)),
                pltpu.SemaphoreType.REGULAR((4,)),
            ],
            compiler_params=pltpu.CompilerParams(
                collective_id=0, has_side_effects=True, vmem_limit_bytes=32 * 2**20
            ),
        )(
            *(
                pltpu.with_memory_space_constraint(x, pltpu.HBM)
                for x in (
                    embedding.T,
                    adagrad_state.reshape(1, ROWS),
                    relation_table.T,
                    source_row,
                    target_row,
                    relation_id,
                    negative_row,
                )
            )
        )
        new_w, new_s = pl.pallas_call(
            write_out,
            out_shape=(pltpu.HBM((COLS, ROWS), F32), pltpu.HBM((1, ROWS), F32)),
            in_specs=[vmem, vmem],
            out_specs=(hbm, hbm),
            scratch_shapes=[dma((2 * N_CH + 1,))],
        )(*(pltpu.with_memory_space_constraint(x, pltpu.VMEM) for x in (new_w, new_s)))
        return new_w.T, new_s.reshape(ROWS)

    in_specs = (
        P("dom", None),
        P("dom"),
        P(),
        P(None, "dom", "edge"),
        P(None, "dom", "edge"),
        P(None, "dom", "edge"),
        P(None, "dom", "edge", None),
    )
    out_specs = (P("dom", None), P("dom"))
    return jax.shard_map(body, mesh=mesh, in_specs=in_specs, out_specs=out_specs, check_vma=False)
```

```python
import functools

import jax
import jax.numpy as jnp
from jax import lax
from jax.experimental import pallas as pl
from jax.experimental.pallas import tpu as pltpu
from jax.sharding import PartitionSpec as P

MESH = pl.DeviceIdType.MESH
F32 = jnp.float32
BF16 = jnp.bfloat16

learning_rate = 0.1
ROWS = 256
HALF = 128
GROUPS = 4
E = 256
COLS = 800

CHUNKS = ((0, 192, 0), (384, 128, 192), (640, 80, 320))
N_CH = len(CHUNKS)
RING = 8
SPANS = ((0, 2), (2, 3))
NATURAL = [(a, n, c) for a, n, c in CHUNKS] + [(a + n, n, c + 400) for a, n, c in CHUNKS]


def chunk(ch):
    a, n, _ = CHUNKS[ch]
    return pl.ds(a, 2 * n)


def parts(ch):
    a, n, _ = CHUNKS[ch]
    return pl.ds(a, n), pl.ds(a + n, n)


def span(j):
    first, last = CHUNKS[SPANS[j][0]], CHUNKS[SPANS[j][1] - 1]
    return pl.ds(first[0], last[0] + 2 * last[1] - first[0])


def dot(a, b, ca, cb):
    return lax.dot_general(a, b, (((ca,), (cb,)), ((), ())), preferred_element_type=F32)


def kernel(
    n_dom,
    emb, state, rel, src, tgt, rid, neg,
    out_w, out_s,
    w, statev, relv, srcv, tgtv, ridv, negv,
    pack, idx, buf, bt, r, q, part, ots, lc, gt, gs, xs, xr,
    load_sem, emb_sem, rel_sem, row_send, row_recv, idx_send, idx_recv, x_send, x_recv, relay,
):
    d = lax.axis_index("dom")
    e = lax.axis_index("edge")
    core = lax.rem(e, 2)
    plane = e - core
    sibling = plane + (1 - core)
    up = [lax.rem(d + k + 1, n_dom) for k in range(2)]
    down = [lax.rem(d + n_dom - k - 1, n_dom) for k in range(2)]
    mine = pl.ds(pl.multiple_of(core * HALF, HALF), HALF)
    other = pl.ds(pl.multiple_of((1 - core) * HALF, HALF), HALF)

    barrier = pltpu.get_barrier_semaphore()

    def tell(dom, edge):
        pl.semaphore_signal(barrier, inc=1, device_id=(dom, edge), device_id_type=MESH)

    @pl.when(core == 0)
    def _():
        tell(down[0], plane)
        tell(d, sibling)
        tell(d, 3 - plane)

    first = lax.rem(d, RING) == 0
    last = lax.rem(d, RING) == RING - 1

    @pl.when(core == 1)
    def _():
        tell(up[0], plane)
        tell(d, plane)
        pl.when(jnp.logical_not(last))(lambda: tell(up[0], 3 - plane))

    index_loads = [
        pltpu.make_async_copy(a, b, load_sem.at[i])
        for i, (a, b) in enumerate(((src, srcv), (tgt, tgtv), (rid, ridv), (neg, negv), (state, statev)))
    ]
    emb_loads = [
        pltpu.make_async_copy(emb.at[pl.ds(c, n), half], w.at[pl.ds(a, n), half], emb_sem.at[j, i])
        for j, half in enumerate((mine, other))
        for i, (a, n, c) in enumerate(NATURAL)
    ]
    rel_loads = [
        pltpu.make_async_copy(rel.at[pl.ds(c, n)], relv.at[pl.ds(a, n)], rel_sem.at[i])
        for i, (a, n, c) in enumerate(NATURAL)
    ]
    for c in index_loads[:4] + emb_loads[: 2 * N_CH]:
        c.start()

    for c in index_loads[:4]:
        c.wait()
    for k in range(2):
        pack[k, 0:1, :] = srcv[k]
        pack[k, 1:2, :] = tgtv[k]
        pack[k, 2:3, :] = ridv[k]
        for j in range(4):
            pack[k, 3 + j : 4 + j, :] = negv[k, 0, :, 256 * j : 256 * (j + 1)]

    order = [lax.rem(plane + o, GROUPS) for o in range(GROUPS)]

    def pass_on(j, dom, edge):
        pl.semaphore_signal(relay.at[j], inc=1, device_id=(dom, edge), device_id_type=MESH)

    for ch in range(N_CH):
        emb_loads[ch].wait()
        emb_loads[N_CH + ch].wait()
        buf[0, core, core, chunk(ch)] = w[chunk(ch), mine].astype(BF16)

    def idx_copy(j, source, target, recv, dom, edge):
        return pltpu.make_async_remote_copy(
            src_ref=source,
            dst_ref=target,
            send_sem=idx_send.at[j],
            recv_sem=idx_recv.at[recv],
            device_id=(dom, edge),
            device_id_type=MESH,
        )

    to_own = idx_copy(0, pack, idx.at[:, e], e, d, plane)
    to_down = idx_copy(1, pack.at[0], idx.at[0, e], e, down[0], plane + 1)
    to_down2 = idx_copy(2, idx.at[1], idx.at[1], 4, down[1], plane + 1)
    across = idx_copy(4, pack, idx.at[:, e], e, d, 2 - plane)
    down_across = idx_copy(3, pack.at[0], idx.at[0, e], e, down[0], 3 - plane)
    both = pl.ds(2 - plane, 2)
    onward = idx_copy(0, idx.at[0, both], idx.at[0, both], 2 - plane, down[0], plane + 1)

    def cross(heard):
        @pl.when(core == 1)
        def _():
            pl.semaphore_wait(barrier, heard)
            pass_on(3, d, sibling)

        pl.when(core == 0)(lambda: pl.semaphore_wait(relay.at[3], 1))
        across.start()

    @pl.when(first)
    def _():
        cross(2)
        pl.when(core == 1)(to_own.start)

    @pl.when(core == 0)
    def _():
        pl.semaphore_wait(barrier, 3)
        pass_on(2, d, sibling)
        pass_on(0, up[0], plane)
        pass_on(0, down[0], plane + 1)

    @pl.when(core == 1)
    def _():
        pl.semaphore_wait(relay.at[2], 1)

    def send_onward():
        for h in (2, 3):
            idx_copy(0, pack, idx.at[:, order[h]], order[h], d, sibling).wait_recv()
        onward.start()

    def idx_wait(k, o):
        g = order[o]

        @pl.when(core == 0)
        def _():
            if k == 0 and o < 2:
                pl.when(e != g)(lambda: idx_copy(0, pack, idx.at[:, g], g, d, sibling).wait_recv())
            elif k == 0 and o == 2:

                @pl.when(jnp.logical_not(first))
                def _():
                    for h in (2, 3):
                        idx_copy(0, pack, idx.at[:, order[h]], order[h], d, sibling).wait_recv()

        @pl.when(core == 1)
        def _():
            if k == 0 and o < 2:
                idx_copy(1, pack.at[0], idx.at[0, g], g, d, sibling).wait_recv()
            elif k == 0 and o == 2:
                pl.when(last)(onward.wait_recv)

                @pl.when(jnp.logical_not(last))
                def _():
                    for h in (2, 3):
                        idx_copy(1, pack.at[0], idx.at[0, order[h]], order[h], d, sibling).wait_recv()
            elif k == 1 and o == 0:
                to_down2.wait_recv()

    def row_copy(k, way, ch):
        return pltpu.make_async_remote_copy(
            src_ref=buf.at[k, core, core, chunk(ch)],
            dst_ref=buf.at[k, 1 - way, core, chunk(ch)],
            send_sem=row_send.at[k, way, ch],
            recv_sem=row_recv.at[k, core, ch],
            device_id=((up[k], plane), (down[k], plane + 1))[way],
            device_id_type=MESH,
        )

    def row_arrival(k, half, ch):
        return pltpu.make_async_remote_copy(
            src_ref=buf.at[k, core, half, chunk(ch)],
            dst_ref=buf.at[k, 1 - core, half, chunk(ch)],
            send_sem=row_send.at[k, half, ch],
            recv_sem=row_recv.at[k, half, ch],
            device_id=(d, sibling),
            device_id_type=MESH,
        )

    def x_copy(k, j):
        return pltpu.make_async_remote_copy(
            src_ref=xs.at[k, span(j)],
            dst_ref=xr.at[k, span(j)],
            send_sem=x_send.at[k, j],
            recv_sem=x_recv.at[k, j],
            device_id=(d, sibling),
            device_id_type=MESH,
        )

    pl.when(jnp.logical_and(core == 1, jnp.logical_not(first)))(to_own.start)
    to_down.start()
    pl.when(jnp.logical_and(core == 0, first))(send_onward)
    for ch in range(N_CH):
        for way in (1, 0):
            row_copy(0, way, ch).start()
        if ch == 0:

            @pl.when(jnp.logical_not(first))
            def _():
                cross(3)
                down_across.start()

    for c in emb_loads[2 * N_CH :] + rel_loads + index_loads[4:]:
        c.start()

    @pl.when(core == 0)
    def _():
        for k in range(2):
            idx[k, e] = pack[k]

    for c in emb_loads[2 * N_CH :]:
        c.wait()
    buf[0, core, 1 - core] = w[:, other].astype(BF16)
    for c in rel_loads + index_loads[4:]:
        c.wait()

    def prepare(k, o):
        idx_wait(k, o)
        g = order[o]
        cols = pl.ds(pl.multiple_of(g * E, E), E)
        at = lax.broadcasted_iota(jnp.int32, (ROWS, E), 0)
        ots[:, cols] = jnp.where(at == idx[k, g, 0:1, :], 1.0, 0.0).astype(BF16)
        count = jnp.zeros((ROWS, E), F32)
        for j in range(4):
            count += jnp.where(at == idx[k, g, 3 + j : 4 + j, :], 1.0, 0.0)
        lc[g] = jnp.log(jnp.sum(count, axis=1, keepdims=True))
        kind = jnp.where(at[:HALF] == idx[k, g, 2:3, :], 1.0, 0.0).astype(BF16)
        r[:, cols] = dot(relv[...], kind, 1, 0).astype(BF16)

    def whole(k, slot, ch):
        return jnp.concatenate([buf[k, slot, half, chunk(ch)] for half in range(2)], axis=1)

    def flip(k, ch):
        for half in range(2):
            bt[half * HALF : (half + 1) * HALF, chunk(ch)] = buf[k, 1, half, chunk(ch)].T

    def products(k, ch, g):
        re, im = parts(ch)
        n = CHUNKS[ch][1]
        cols = pl.ds(pl.multiple_of(g * E, E), E)
        s = dot(whole(k, 0, ch), ots[:, cols], 1, 0)
        rr = r[re, cols].astype(F32)
        ri = r[im, cols].astype(F32)
        q[re, cols] = (s[:n] * rr - s[n:] * ri).astype(BF16)
        q[im, cols] = (s[:n] * ri + s[n:] * rr).astype(BF16)

    def scores(ch):
        for g in range(GROUPS):
            cols = slice(g * E, (g + 1) * E)
            new = dot(bt[:, chunk(ch)], q[chunk(ch), cols], 1, 0)
            part[:, cols] = new if ch == 0 else part[:, cols] + new

    def pulls(k):
        at = lax.broadcasted_iota(jnp.int32, (ROWS, E), 0)
        for g in range(GROUPS):
            cols = slice(g * E, (g + 1) * E)
            score = part[:, cols] + dot(bt[:, chunk(N_CH - 1)], q[chunk(N_CH - 1), cols], 1, 0)
            hit = at == idx[k, g, 1:2, :]
            pos = jnp.sum(jnp.where(hit, score, 0.0), axis=0, keepdims=True)
            z = score + lc[g]
            top = jnp.maximum(jnp.max(z, axis=0, keepdims=True), pos)
            ez = jnp.exp(z - top)
            ep = jnp.exp(pos - top)
            inv = 1.0 / (jnp.sum(ez, axis=0, keepdims=True) + ep)
            pull = ep * inv - 1.0
            gt[:, cols] = (ez * inv + jnp.where(hit, pull, 0.0)).astype(BF16)

    def source_terms(k, ch):
        re, im = parts(ch)
        n = CHUNKS[ch][1]
        for g in range(GROUPS):
            cols = slice(g * E, (g + 1) * E)
            gq = dot(whole(k, 1, ch), gt[:, cols], 1, 0).astype(BF16)
            rr, ri = r[re, cols], r[im, cols]
            gs[re, cols] = gq[:n] * rr + gq[n:] * ri
            gs[im, cols] = gq[n:] * rr - gq[:n] * ri

    def squares(k, j):
        g = xs[k, span(j)].astype(F32) + xr[k, span(j)].astype(F32)
        return jnp.sum(g * g, axis=0, keepdims=True)

    def update(k, half, lane):
        g = xs[k, :, lane].astype(F32) + xr[k, :, lane].astype(F32)
        new_w = w[:, lane] - g * (learning_rate * lax.rsqrt(statev[:, lane]))
        if k == 0:
            w[:, lane] = new_w
            buf[1, core, half] = new_w.astype(BF16)
        else:
            out_w[:, lane] = new_w

    for k in range(2):
        for o in range(GROUPS):
            prepare(k, o)

            @pl.when(core == 0)
            def _():
                for ch in range(N_CH):
                    products(k, ch, order[o])

        @pl.when(core == 1)
        def _():
            for ch in range(N_CH):
                flip(k, ch)

        for ch in range(N_CH):
            for half in range(2):
                row_arrival(k, half, ch).wait_recv()
            pl.when(core == 0)(lambda: flip(k, ch))

            @pl.when(core == 1)
            def _():
                for g in range(GROUPS):
                    products(k, ch, g)

            if ch < N_CH - 1:
                scores(ch)
        if k == 0:
            pl.semaphore_wait(relay.at[0], 1)
            pass_on(1, d, sibling)
            pl.when(core == 0)(to_down2.start)
        pulls(k)
        for j in range(2):

            @pl.when(core == 0)
            def _():
                for ch in range(*SPANS[j]):
                    source_terms(k, ch)
                xs[k, span(j)] = dot(gs[span(j), :], ots[...], 1, 1).astype(BF16)

            @pl.when(core == 1)
            def _():
                xs[k, span(j)] = dot(q[span(j), :], gt[...], 1, 1).astype(BF16)

            x_copy(k, j).start()
        total = jnp.zeros((1, ROWS), F32)
        for j in range(2):
            x_copy(k, j).wait_recv()
            total += squares(k, j)
        statev[...] = statev[...] + total * (1.0 / COLS)
        if k == 1:
            out_s[...] = statev[...]
        update(k, core, mine)
        if k == 0:
            pl.semaphore_wait(relay.at[1], 1)
            for ch in range(N_CH):
                for way in range(2):
                    row_copy(1, way, ch).start()
        update(k, 1 - core, other)

    to_down.wait_send()
    across.wait_send()
    pl.when(jnp.logical_not(first))(down_across.wait_send)

    @pl.when(core == 0)
    def _():
        to_down2.wait_send()
        pl.when(first)(onward.wait_send)

    @pl.when(core == 1)
    def _():
        to_own.wait_send()

    for k in range(2):
        for j in range(2):
            x_copy(k, j).wait_send()
        for ch in range(N_CH):
            for way in range(2):
                row_copy(k, way, ch).wait_send()


def write_out(w, s, out_w, out_s, sem):
    copies = [
        pltpu.make_async_copy(w.at[pl.ds(a, n)], out_w.at[pl.ds(c, n)], sem.at[i])
        for i, (a, n, c) in enumerate(NATURAL)
    ]
    copies.append(pltpu.make_async_copy(s, out_s, sem.at[2 * N_CH]))
    for c in copies:
        c.start()
    for c in copies:
        c.wait()


def solution(mesh):
    n_dom = mesh.shape["dom"]

    def body(embedding, adagrad_state, relation_table, source_row, target_row, relation_id, negative_row):
        vmem = pl.BlockSpec(memory_space=pltpu.VMEM)
        hbm = pl.BlockSpec(memory_space=pltpu.HBM)
        dma = pltpu.SemaphoreType.DMA
        new_w, new_s = pl.pallas_call(
            functools.partial(kernel, n_dom),
            out_shape=(pltpu.VMEM((COLS, ROWS), F32), pltpu.VMEM((1, ROWS), F32)),
            in_specs=[hbm] * 7,
            out_specs=(vmem, vmem),
            scratch_shapes=[
                pltpu.VMEM((COLS, ROWS), F32),
                pltpu.VMEM((1, ROWS), F32),
                pltpu.VMEM((COLS, 128), BF16),
                pltpu.VMEM(source_row.shape, jnp.int32),
                pltpu.VMEM(target_row.shape, jnp.int32),
                pltpu.VMEM(relation_id.shape, jnp.int32),
                pltpu.VMEM(negative_row.shape, jnp.int32),
                pltpu.VMEM((2, 8, E), jnp.int32),
                pltpu.VMEM((2, GROUPS, 8, E), jnp.int32),
                pltpu.VMEM((2, 2, 2, COLS, HALF), BF16),
                pltpu.VMEM((ROWS, COLS), BF16),
                pltpu.VMEM((COLS, GROUPS * E), BF16),
                pltpu.VMEM((COLS, GROUPS * E), BF16),
                pltpu.VMEM((ROWS, GROUPS * E), F32),
                pltpu.VMEM((ROWS, GROUPS * E), BF16),
                pltpu.VMEM((GROUPS, ROWS, 1), F32),
                pltpu.VMEM((ROWS, GROUPS * E), BF16),
                pltpu.VMEM((COLS, GROUPS * E), BF16),
                pltpu.VMEM((2, COLS, ROWS), BF16),
                pltpu.VMEM((2, COLS, ROWS), BF16),
                dma((5,)),
                dma((2, 2 * N_CH)),
                dma((2 * N_CH,)),
                dma((2, 2, N_CH)),
                dma((2, 2, N_CH)),
                dma((5,)),
                dma((5,)),
                dma((2, 2)),
                dma((2, 2)),
                pltpu.SemaphoreType.REGULAR((4,)),
            ],
            compiler_params=pltpu.CompilerParams(
                collective_id=0, has_side_effects=True, vmem_limit_bytes=32 * 2**20
            ),
        )(
            *(
                pltpu.with_memory_space_constraint(x, pltpu.HBM)
                for x in (
                    embedding.T,
                    adagrad_state.reshape(1, ROWS),
                    relation_table.T,
                    source_row,
                    target_row,
                    relation_id,
                    negative_row,
                )
            )
        )
        new_w, new_s = pl.pallas_call(
            write_out,
            out_shape=(pltpu.HBM((COLS, ROWS), F32), pltpu.HBM((1, ROWS), F32)),
            in_specs=[vmem, vmem],
            out_specs=(hbm, hbm),
            scratch_shapes=[dma((2 * N_CH + 1,))],
        )(*(pltpu.with_memory_space_constraint(x, pltpu.VMEM) for x in (new_w, new_s)))
        return new_w.T, new_s.reshape(ROWS)

    in_specs = (
        P("dom", None),
        P("dom"),
        P(),
        P(None, "dom", "edge"),
        P(None, "dom", "edge"),
        P(None, "dom", "edge"),
        P(None, "dom", "edge", None),
    )
    out_specs = (P("dom", None), P("dom"))
    return jax.shard_map(body, mesh=mesh, in_specs=in_specs, out_specs=out_specs, check_vma=False)
```
